256 devices in a mesh: patch: 8 (over y, core), visit: 32 (over x, z).
Axes of the slice: x: 4, y: 4, z: 8, core: 2. Of those that a mesh axis runs over, the one named last changes fastest.
Arguments:
- images: bfloat16 [8192, 128, 128], P(('patch', 'visit')), may hold values from -6 to 6
- variances: bfloat16 [8192, 128, 128], P(('patch', 'visit')), may hold values from 0.5 to 4
- bad_pixels: int32 [8192, 128, 128], P(('patch', 'visit')), may hold values 0 or 1
- routes: int32 [8192, 1], P(('patch', 'visit')), may hold values from 0 to 7; in each aligned block of 32 rows (0 to 31, 32 to 63, ...) at most 8 rows name the same one
- offsets: int32 [8192, 2], P(('patch', 'visit')), may hold values from 0 to 112
- tile_visits: int32 [8192], P(('patch', 'visit')), may hold values from 0 to 1
- coefficients: bfloat16 [64, 3, 16], P('visit'), may hold values from -1.5 to 1.5
- kernel_counts: int32 [64], P('visit'), may hold values from 1 to 16
- taps: bfloat16 [16, 2, 41], replicated, may hold values from -0.796875 to 0.796875
Outputs:
- coadd: float32 [8192, 1024], P(('patch', 'visit'))
- depth: float32 [8192, 1024], P(('patch', 'visit'))
The draws below stay inside these ranges and needn't reach their ends.
Inputs may be any that keep to these rules, and one draw needn't show every extreme that they name: `routes`: in the rows of one device at most 8 tiles intersect one patch, and exactly 8 intersect one patch on some device.
All inputs are finite; a program needn't handle non-finite values. No bound on the sum of `bad_pixels` on one device may be relied on, other than what follows from the above.
Results may differ from the reference program's by a relative error of at most 0.0046.
Values may be sent and summed in bfloat16 or wider, within the bound.
A program may use at most 64 MiB of HBM per device.

```python
import math
import jax
import jax.numpy as jnp
import numpy as np
from jax import lax

TS = 128
TAPS = 41
NBASIS = 16
VIS_DEV = 2
WIN = 1024
TILES_DEV = 32
CAP = 8
VISITS = 64
TILES = 8192
N_PATCH = 8
N_VISIT = 32


def place_ends(result, key, smallest, top_value):
    longest = result.shape.index(max(result.shape))
    spots = []
    for shift in (0, 1):
        where = [jax.random.randint(jax.random.fold_in(key, axis), (), 0, length) for axis, length in enumerate(result.shape)]
        where[longest] = (where[longest] + shift) % result.shape[longest]
        spots.append(tuple(where))
    return result.at[spots[0]].set(smallest).at[spots[1]].set(top_value)


def shard_levels(stream_key, dims, pieces, low, high):
    def one(dim, parts):
        draws = jax.random.uniform(jax.random.fold_in(jax.random.fold_in(stream_key, 6), dim), (parts,), jnp.float32, low / len(pieces), high / len(pieces))
        return jnp.repeat(jnp.exp(draws), dims[dim] // parts).reshape((-1,) + (1,) * (len(dims) - dim - 1))

    factor_of = one(*pieces[0])
    for cut in pieces[1:]:
        factor_of = factor_of * one(*cut)
    return factor_of


def shared_out(own_key, own, number, rows, amount, top, bound, skew):
    sequence = jax.random.permutation(own_key, amount)
    heavy_load, common = portions_of(amount, rows * top, bound, skew, True), portions_of(amount, rows * top, bound, skew, False)
    places = jnp.arange(amount)

    def named(lengths, turn):
        used = int((lengths > 0).sum())
        fixed = max(1, used // 4)
        passed = fixed + (places - fixed + turn * (used - fixed)) % max(1, amount - fixed)
        return jnp.zeros((amount,), jnp.int32).at[sequence[jnp.where(places < fixed, places, passed)]].set(jnp.asarray(lengths, jnp.int32))

    lengths = jnp.where(number % 4 == 0, named(heavy_load, number // 4), named(common, number - number // 4 - 1))
    mixed = jax.random.permutation(jax.random.fold_in(own, 3), amount)
    giver, sink = mixed[0:amount // 2 * 2:2], mixed[1:amount // 2 * 2:2]
    room = jnp.minimum(lengths[giver] - 1, bound - lengths[sink]) // 2
    room = jnp.where((giver == sequence[0]) | (sink == sequence[0]) | (lengths[sink] == 0), 0, jnp.maximum(room, 0))
    passed = jax.random.randint(jax.random.fold_in(own, 4), (amount // 2,), 0, 1 << 20) % (room + 1)
    lengths = lengths.at[giver].add(-passed).at[sink].add(passed)
    members = jnp.searchsorted(jnp.cumsum(lengths), jnp.arange(rows * top), side="right").astype(jnp.int32)
    listing = members.reshape(top, rows).T
    listing = listing[jax.random.permutation(jax.random.fold_in(own, 1), rows)]
    turn = jax.random.randint(jax.random.fold_in(own, 2), (rows, 1), 0, top)
    return jnp.take_along_axis(listing, (jnp.arange(top)[None, :] + turn) % top, axis=1)


def portions_of(number_of, total, limit, skew, full):
    portions = [(1 << 20) // math.isqrt(rank ** skew) + 1 for rank in range(1, number_of + 1)]
    largest = limit if full else min(limit, max(-(-total // number_of), total * portions[0] // sum(portions)))
    least = 1 if total - largest >= number_of - 1 else 0
    holding, spare = [largest] + [least] * (number_of - 1), total - largest - least * (number_of - 1)
    while spare > 0:
        movable = [i for i in range(1, number_of) if holding[i] < largest] or [i for i in range(1, number_of) if holding[i] < limit]
        whole, budget = sum([portions[i] for i in movable]), spare
        for i in movable:
            extra = min(limit - holding[i], max(1, budget * portions[i] // whole), spare)
            holding[i] = holding[i] + extra
            spare = spare - extra
    return np.array(holding)


def bell_draw(stream_key, shape, spread, bound, cuts=(), held_as=jnp.bfloat16):
    entries = jax.random.normal(stream_key, shape, jnp.float32) * spread
    if len(cuts) > 0:
        entries = shard_levels(stream_key, shape, cuts, -0.22, 0.18) * entries
    return jnp.clip(entries, min=-bound, max=bound).astype(held_as)


def setup_inputs(seed: int = 0) -> dict:
    keys = jax.random.split(jax.random.key(seed), 10)
    images = bell_draw(keys[0], (TILES, TS, TS), 1.0, 6.0, ((0, 256),))
    variances = jnp.clip(jnp.exp(math.log(4.0) - 2.0794415 * jax.random.uniform(keys[1], (TILES, TS, TS), jnp.float32) ** shard_levels(keys[1], (TILES, TS, TS), ((0, 256),), -0.2, 0.2)), 0.5, 4.0).astype(jnp.bfloat16)
    bad_pixels = place_ends((jax.random.randint(keys[2], (TILES, TS, TS), 0, 10) < 1).astype(jnp.int32), jax.random.fold_in(keys[2], 1), 0, 1)
    routes_keys = jax.random.split(jax.random.fold_in(keys[3], 1), TILES // TILES_DEV)
    routes_turns = jax.random.permutation(jax.random.fold_in(keys[3], 3), TILES // TILES_DEV)
    routes = jax.vmap(lambda own, number: shared_out(jax.random.fold_in(keys[3], 2), own, number, TILES_DEV, N_PATCH, 1, CAP, 2))(routes_keys, routes_turns).reshape((TILES, 1))
    offsets = place_ends(jax.random.randint(keys[4], (TILES, 2), 0, (WIN - TS) // 8 + 1), jax.random.fold_in(keys[4], 1), 0, ((WIN - TS) // 8 + 1) - 1).astype(jnp.int32)
    tile_visits = place_ends(jax.random.randint(keys[5], (TILES,), 0, VIS_DEV), jax.random.fold_in(keys[5], 1), 0, VIS_DEV - 1).astype(jnp.int32)
    coefficients = bell_draw(keys[6], (VISITS, 3, NBASIS), 0.25, 1.5, ((0, 32),))
    kernel_counts = place_ends(jax.random.randint(keys[7], (VISITS,), 1, NBASIS + 1), jax.random.fold_in(keys[7], 1), 1, NBASIS).astype(jnp.int32)
    taps = bell_draw(keys[8], (NBASIS, 2, TAPS), 0.16, 0.796875)
    return dict(images=images, variances=variances, bad_pixels=bad_pixels, routes=routes, offsets=offsets, tile_visits=tile_visits, coefficients=coefficients, kernel_counts=kernel_counts, taps=taps)


def band_matrices(taps, tile_side):
    tap_span = taps.shape[2]
    grid = (tap_span, tile_side, tile_side)
    tap_index = lax.broadcasted_iota(jnp.int32, grid, 0)
    row_iota = lax.broadcasted_iota(jnp.int32, grid, 1)
    col_iota = lax.broadcasted_iota(jnp.int32, grid, 2)
    lookup = (col_iota - row_iota + tap_span // 2 == tap_index).astype(jnp.float32)
    taps_wide = taps.astype(jnp.float32)
    vertical = jnp.einsum("kt,tij->kij", taps_wide[:, 0, :], lookup, precision=lax.Precision.HIGHEST).astype(jnp.bfloat16)
    horizontal = jnp.einsum("kt,tij->kij", taps_wide[:, 1, :], lookup, precision=lax.Precision.HIGHEST).astype(jnp.bfloat16)
    return vertical, horizontal


def match_tiles(images, tile_coefs, anchors, vertical, horizontal):
    tile_side = images.shape[1]
    pixel_iota = lax.iota(jnp.float32, tile_side)
    vertical_wide = vertical.astype(jnp.float32)
    horizontal_wide = horizontal.astype(jnp.float32)

    def match_single(image, coefs, anchor):
        blurred = jnp.einsum("kij,jw->kiw", vertical_wide, image.astype(jnp.float32), precision=lax.Precision.HIGHEST).astype(jnp.bfloat16)
        blurred = lax.optimization_barrier(blurred)
        smoothed = jnp.einsum("kiw,kvw->kiv", blurred.astype(jnp.float32), horizontal_wide, precision=lax.Precision.HIGHEST)
        terms = jnp.einsum("ck,kiv->civ", coefs, smoothed, precision=lax.Precision.HIGHEST)
        row_place = (anchor[0] + pixel_iota) / WIN
        col_place = (anchor[1] + pixel_iota) / WIN
        matched = terms[0] + row_place[:, None] * terms[1] + col_place[None, :] * terms[2]
        return matched.astype(jnp.bfloat16)

    return jax.vmap(match_single)(images, tile_coefs, anchors)


def reference(images, variances, bad_pixels, routes, offsets, tile_visits, coefficients, kernel_counts, taps):
    vertical, horizontal = band_matrices(taps, TS)
    active = (jnp.arange(NBASIS, dtype=jnp.int32)[None, :] < kernel_counts[:, None]).astype(jnp.float32)
    visit_coefs = coefficients.astype(jnp.float32) * active[:, None, :]
    weights = jnp.where(bad_pixels == 0, 1.0 / variances.astype(jnp.float32), 0.0).astype(jnp.bfloat16)

    def block_step(block, sums):
        start = (block * TILES_DEV).astype(jnp.int32)
        block_images = lax.dynamic_slice_in_dim(images, start, TILES_DEV, 0)
        block_weights = lax.dynamic_slice_in_dim(weights, start, TILES_DEV, 0)
        block_routes = lax.dynamic_slice_in_dim(routes, start, TILES_DEV, 0)
        block_offsets = lax.dynamic_slice_in_dim(offsets, start, TILES_DEV, 0)
        block_visits = lax.dynamic_slice_in_dim(tile_visits, start, TILES_DEV, 0)
        group = block % N_VISIT
        visit_ids = (group * VIS_DEV + block_visits).astype(jnp.int32)
        tile_coefs = visit_coefs[visit_ids]
        anchors = (8 * block_offsets).astype(jnp.float32)
        matched = match_tiles(block_images, tile_coefs, anchors, vertical, horizontal)

        def add_tile(position, inner):
            numer, denom = inner
            target = block_routes[position, 0].astype(jnp.int32)
            top = (8 * block_offsets[position, 0]).astype(jnp.int32)
            left = (8 * block_offsets[position, 1]).astype(jnp.int32)
            weight_tile = block_weights[position].astype(jnp.float32)[None]
            value_tile = matched[position].astype(jnp.float32)[None]
            corner = (target, top, left)
            numer = lax.dynamic_update_slice(numer, lax.dynamic_slice(numer, corner, (1, TS, TS)) + weight_tile * value_tile, corner)
            denom = lax.dynamic_update_slice(denom, lax.dynamic_slice(denom, corner, (1, TS, TS)) + weight_tile, corner)
            return numer, denom

        return lax.fori_loop(0, TILES_DEV, add_tile, sums)

    empty = jnp.zeros((N_PATCH, WIN, WIN), jnp.float32)
    numer, denom = lax.fori_loop(0, N_PATCH * N_VISIT, block_step, (empty, empty))
    coadd = numer / jnp.maximum(denom, 1.0)
    return coadd.reshape(N_PATCH * WIN, WIN), denom.reshape(N_PATCH * WIN, WIN)
```

```python
import functools

import jax
import jax.numpy as jnp
from jax import lax
from jax.experimental import pallas as pl
from jax.experimental.pallas import tpu as pltpu
from jax.sharding import PartitionSpec as P

TS = 128
WIN = 1024
CAP = 8
NB = 16
NT = 32
NP = 8
NX = 4
NZ = 8
ROWS = 32
HALF = WIN // 2
MESH = pl.DeviceIdType.MESH
BF16 = jnp.bfloat16
F32 = jnp.float32
VMEM = pl.BlockSpec(memory_space=pltpu.VMEM)
SMEM = pl.BlockSpec(memory_space=pltpu.SMEM)
ANY = pl.BlockSpec(memory_space=pl.ANY)


def band(row):
    wide = jnp.broadcast_to(row, (TS, 2 * TS))
    return pltpu.roll(wide, 0, 1, stride=1, stride_axis=0)[:, :TS].astype(BF16)


def greet(axis, others):
    barrier = pltpu.get_barrier_semaphore()
    for other in others:
        pl.semaphore_signal(barrier, inc=1, device_id={axis: other}, device_id_type=MESH)


def front_kernel(
    table, coefs, rolls, meta, img_in, var_in, bad_in, wgt_out, mat_out, meta_out,
    img, var, bad, wslots, tiles, vert, horz, lm, in_sem, own_sem, send_sem, recv_sem,
):
    me = lax.axis_index("patch")
    loads = [
        pltpu.make_async_copy(src, dst, in_sem.at[i])
        for i, (src, dst) in enumerate(((var_in, var), (bad_in, bad), (img_in, img)))
    ]
    for load in loads:
        load.start()
    greet("patch", [lax.rem(me + d, NP) for d in range(1, NP)])
    pl.semaphore_wait(pltpu.get_barrier_semaphore(), NP - 1)
    loads[0].wait()
    loads[1].wait()

    def weigh(j, carry):
        t = table[j]
        weight = jnp.where(bad[t] == 0, 1.0 / var[t].astype(F32), 0.0)
        wslots[j] = weight.astype(BF16)
        return carry

    copies = []
    for d in (4, 3, 5, 2, 6, 1, 7, 0):
        there = lax.rem(me + d, NP)
        lax.fori_loop(there * CAP, there * CAP + CAP, weigh, 0)
        block = wslots.at[pl.ds(there * CAP, CAP)]
        if d == 0:
            own = [
                pltpu.make_async_copy(block, wgt_out.at[me], own_sem.at[0]),
                pltpu.make_async_copy(meta.at[me], meta_out.at[me], own_sem.at[1]),
            ]
            for c in own:
                c.start()
            continue
        for i, (src, dst) in enumerate(((meta.at[there], meta_out), (block, wgt_out))):
            copies.append(
                pltpu.make_async_remote_copy(
                    src_ref=src,
                    dst_ref=dst.at[me],
                    send_sem=send_sem.at[i, d],
                    recv_sem=recv_sem.at[i, d],
                    device_id={"patch": there},
                    device_id_type=MESH,
                )
            )
            copies[-1].start()

    horz[...] = jnp.zeros_like(horz)
    for k in range(NB):
        vert[k * TS : (k + 1) * TS, :] = band(rolls[k : k + 1, :])
        half = slice((k % 2) * TS, (k % 2 + 1) * TS)
        horz[k // 2, half, half] = band(rolls[NB + k : NB + k + 1, :])
    loads[2].wait()

    row_iota = lax.broadcasted_iota(jnp.int32, (TS, TS), 0)
    col_iota = lax.broadcasted_iota(jnp.int32, (1, TS), 1)

    def pair(step, carry):
        two = jnp.concatenate([img[2 * step], img[2 * step + 1]], axis=1)
        bases = [table[128 + 2 * step + i] * (3 * NB) for i in range(2)]
        rho = [(row_iota + 8 * table[64 + 4 * step + 2 * i]).astype(F32) * (1.0 / WIN) for i in range(2)]
        gamma = [(col_iota + 8 * table[65 + 4 * step + 2 * i]).astype(F32) * (1.0 / WIN) for i in range(2)]
        for part in range(NB // 4):
            blurred = jnp.dot(
                vert[part * 4 * TS : (part + 1) * 4 * TS, :], two, preferred_element_type=F32
            )
            for kk in range(4):
                k = part * 4 + kk
                for i in range(2):
                    lm[i * TS : (i + 1) * TS, k * TS : (k + 1) * TS] = blurred[
                        kk * TS : (kk + 1) * TS, i * TS : (i + 1) * TS
                    ].astype(BF16)
        matched = [None, None]
        for kp in range(NB // 2):
            smooth = jnp.dot(lm[:, kp * 2 * TS : (kp + 1) * 2 * TS], horz[kp], preferred_element_type=F32)
            for kk in range(2):
                k = 2 * kp + kk
                for i in range(2):
                    a0 = coefs[bases[i] + k]
                    a1 = coefs[bases[i] + NB + k]
                    a2 = coefs[bases[i] + 2 * NB + k]
                    term = ((a0 + a1 * rho[i]) + a2 * gamma[i]) * smooth[
                        i * TS : (i + 1) * TS, kk * TS : (kk + 1) * TS
                    ]
                    matched[i] = term if matched[i] is None else matched[i] + term
        for i in range(2):
            tiles[2 * step + i] = matched[i].astype(BF16)
        return carry

    lax.fori_loop(0, NT // 2, pair, 0)

    def sort(j, carry):
        mat_out[j] = tiles[table[j]]
        return carry

    lax.fori_loop(0, NP * CAP, sort, 0)
    for c in own:
        c.wait()
    for c in copies:
        c.wait()


def front(table, coefs, rolls, meta, img, var, bad):
    dma = pltpu.SemaphoreType.DMA
    return pl.pallas_call(
        front_kernel,
        out_shape=(
            jax.ShapeDtypeStruct((NP, CAP, TS, TS), BF16),
            jax.ShapeDtypeStruct((NP * CAP, TS, TS), BF16),
            jax.ShapeDtypeStruct((NP, CAP, TS), jnp.int32),
        ),
        in_specs=[SMEM, SMEM, VMEM, ANY, ANY, ANY, ANY],
        out_specs=(ANY, VMEM, ANY),
        scratch_shapes=[
            pltpu.VMEM((NT, TS, TS), BF16),
            pltpu.VMEM((NT, TS, TS), BF16),
            pltpu.VMEM((NT, TS, TS), jnp.int32),
            pltpu.VMEM((NP * CAP, TS, TS), BF16),
            pltpu.VMEM((NT, TS, TS), BF16),
            pltpu.VMEM((NB * TS, TS), BF16),
            pltpu.VMEM((NB // 2, 2 * TS, 2 * TS), BF16),
            pltpu.VMEM((2 * TS, NB * TS), BF16),
            dma((3,)), dma((2,)), dma((2, NP)), dma((2, NP)),
        ],
        compiler_params=pltpu.CompilerParams(
            collective_id=0, has_side_effects=True, vmem_limit_bytes=40 * 2**20
        ),
        name="match_tiles",
    )(table, coefs, rolls, meta, img, var, bad)


def add_kernel(count, meta, *refs):
    tiles, (by_z, by_x, window) = refs[:count], refs[count:]
    source = pl.program_id(0)

    @pl.when(source == 0)
    def _():
        def clear(i, carry):
            window[i] = jnp.zeros((WIN, TS), F32)
            return carry

        lax.fori_loop(0, WIN // TS + 1, clear, 0)

    lane = lax.broadcasted_iota(jnp.int32, (TS, TS), 1)

    def add(s, carry):
        j = source * CAP + s

        @pl.when(meta[j, 2] > 0)
        def _():
            top = pl.multiple_of(meta[j, 0], 8)
            left = meta[j, 1]
            q = left // TS
            shift = lax.rem(left, TS)
            tile = tiles[0][s].astype(F32)
            for other in tiles[1:]:
                tile = tile * other[s].astype(F32)
            tile = pltpu.roll(tile, shift, 1)
            right_part = lane >= shift
            window[q, pl.ds(top, TS), :] += jnp.where(right_part, tile, 0.0)
            window[q + 1, pl.ds(top, TS), :] += jnp.where(right_part, 0.0, tile)

        return carry

    lax.fori_loop(0, CAP, add, 0)

    @pl.when(source == NP - 1)
    def _():
        def write(v, carry):
            x = v // NZ
            z = lax.rem(v, NZ)
            at = pl.multiple_of(v * ROWS, ROWS)
            for q in range(WIN // TS // 2):
                cols = slice(q * TS, (q + 1) * TS)
                by_z[z, x, :, cols] = window[q, pl.ds(at, ROWS), :].astype(BF16)
                by_x[x, z, :, cols] = window[q + WIN // TS // 2, pl.ds(at, ROWS), :].astype(BF16)
            return carry

        lax.fori_loop(0, NX * NZ, write, 0)


def add_tiles(meta, *tiles):
    block = pl.BlockSpec((CAP, TS, TS), lambda i: (i, 0, 0))
    return pl.pallas_call(
        functools.partial(add_kernel, len(tiles)),
        grid=(NP,),
        out_shape=(
            jax.ShapeDtypeStruct((NZ, NX, ROWS, HALF), BF16),
            jax.ShapeDtypeStruct((NX, NZ, ROWS, HALF), BF16),
        ),
        in_specs=[SMEM] + [block] * len(tiles),
        out_specs=(VMEM, VMEM),
        scratch_shapes=[pltpu.VMEM((WIN // TS + 1, WIN, TS), F32)],
        compiler_params=pltpu.CompilerParams(vmem_limit_bytes=40 * 2**20),
        name="add_tiles",
    )(meta, *(t.reshape(NP * CAP, TS, TS) for t in tiles))


class Ring:
    def __init__(self, n, me, device, src, send, recv, send_sem, recv_sem):
        self.n, self.me, self.device, self.src = n, me, device, src
        self.send, self.recv, self.send_sem, self.recv_sem = send, recv, send_sem, recv_sem
        self.copies = {}
        self.mid = src.shape[1] // 2

    def start(self, way, j):
        n, mid = self.n, self.mid
        to = lax.rem(self.me + (1 if way == 0 else n - 1), n)
        far = n // 2 - j
        owner = lax.rem(self.me + (far if way == 0 else n - far), n)
        own, other = (slice(0, mid), slice(mid, 2 * mid)) if way == 0 else (slice(mid, 2 * mid), slice(0, mid))
        if j == 0:
            src, dst = self.src.at[owner, own], self.recv.at[way, 0, own]
        else:
            got = self.recv.at[way, j - 1]
            self.copies[way, j - 1].wait_recv()
            dst, src = self.recv.at[way, j], self.send.at[way, j]
            block = self.src.at[owner]
            src[own] = (block[own].astype(F32) + got[own].astype(F32)).astype(BF16)
            if j == 1:
                src[other] = block[other]
            else:
                src[other] = (block[other].astype(F32) + got[other].astype(F32)).astype(BF16)
        copy = pltpu.make_async_remote_copy(
            src_ref=src,
            dst_ref=dst,
            send_sem=self.send_sem.at[way, j],
            recv_sem=self.recv_sem.at[way, j],
            device_id={"visit": self.device(to)},
            device_id_type=MESH,
        )
        copy.start()
        self.copies[way, j] = copy

    def total(self):
        last = self.n // 2 - 1
        for way in range(2):
            self.copies[way, last].wait_recv()
        return (
            self.src[self.me].astype(F32)
            + self.recv[0, last].astype(F32)
            + self.recv[1, last].astype(F32)
        )

    def finish(self):
        for copy in self.copies.values():
            copy.wait_send()


class Direct:
    def __init__(self, n, me, device, src, recv, send_sem, recv_sem):
        self.n, self.me, self.src, self.recv = n, me, src, recv
        self.copies = []
        for d in range(1, n):
            to = lax.rem(me + d, n)
            self.copies.append(
                pltpu.make_async_remote_copy(
                    src_ref=src.at[to],
                    dst_ref=recv.at[d],
                    send_sem=send_sem.at[d],
                    recv_sem=recv_sem.at[d],
                    device_id={"visit": device(to)},
                    device_id_type=MESH,
                )
            )
            self.copies[-1].start()

    def total(self):
        out = self.src[self.me].astype(F32)
        for d in range(1, self.n):
            self.copies[d - 1].wait_recv()
            out = out + self.recv[d].astype(F32)
        return out

    def finish(self):
        for copy in self.copies:
            copy.wait_send()


def place():
    me = lax.axis_index("visit")
    x, z = me // NZ, lax.rem(me, NZ)
    return x, z, lambda to: x * NZ + to, lambda to: to * NZ + z


def greet_groups():
    x, z, along_z, along_x = place()
    greet("visit", [along_z(lax.rem(z + d, NZ)) for d in range(1, NZ)])
    greet("visit", [along_x(lax.rem(x + d, NX)) for d in range(1, NX)])
    return NZ + NX - 2


def sum_groups(
    by_z, by_x, finish,
    z_send, z_recv, x_send, x_recv, z_mid, x_mid, z_got, x_got,
    zs_sem, zr_sem, xs_sem, xr_sem, zds_sem, zdr_sem, xds_sem, xdr_sem,
):
    x, z, along_z, along_x = place()
    ring_z = Ring(NZ, z, along_z, by_z, z_send, z_recv, zs_sem, zr_sem)
    ring_x = Ring(NX, x, along_x, by_x, x_send, x_recv, xs_sem, xr_sem)
    for j in range(2):
        for way in range(2):
            ring_z.start(way, j)
            ring_x.start(way, j)
    ring_z.start(0, 2)
    ring_z.start(1, 2)
    x_mid[...] = ring_x.total().astype(BF16)
    direct_z = Direct(NZ, z, along_z, x_mid, z_got, zds_sem, zdr_sem)
    ring_z.start(0, 3)
    ring_z.start(1, 3)
    z_mid[...] = ring_z.total().astype(BF16)
    direct_x = Direct(NX, x, along_x, z_mid, x_got, xds_sem, xdr_sem)
    finish(slice(HALF, WIN), direct_z.total())
    finish(slice(0, HALF), direct_x.total())
    for part in (ring_z, ring_x, direct_z, direct_x):
        part.finish()


def sum_scratch():
    z_block, x_block = (NX, ROWS, HALF), (NZ, ROWS, HALF)
    dma = pltpu.SemaphoreType.DMA
    return [
        pltpu.VMEM((2, NZ // 2) + z_block, BF16),
        pltpu.VMEM((2, NZ // 2) + z_block, BF16),
        pltpu.VMEM((2, NX // 2) + x_block, BF16),
        pltpu.VMEM((2, NX // 2) + x_block, BF16),
        pltpu.VMEM(z_block, BF16),
        pltpu.VMEM(x_block, BF16),
        pltpu.VMEM((NZ, ROWS, HALF), BF16),
        pltpu.VMEM((NX, ROWS, HALF), BF16),
        dma((2, NZ // 2)), dma((2, NZ // 2)), dma((2, NX // 2)), dma((2, NX // 2)),
        dma((NZ,)), dma((NZ,)), dma((NX,)), dma((NX,)),
    ]


def middle_kernel(mat, by_z, by_x, mat_out, depth, own_sem, send_sem, recv_sem, *scratch):
    me = lax.axis_index("patch")
    greet("patch", [lax.rem(me + d, NP) for d in range(1, NP)])
    number = greet_groups() + NP - 1
    pl.semaphore_wait(pltpu.get_barrier_semaphore(), number)
    copies = []
    for d in (4, 3, 5, 2, 6, 1, 7):
        there = lax.rem(me + d, NP)
        copies.append(
            pltpu.make_async_remote_copy(
                src_ref=mat.at[there],
                dst_ref=mat_out.at[me],
                send_sem=send_sem.at[d],
                recv_sem=recv_sem.at[d],
                device_id={"patch": there},
                device_id_type=MESH,
            )
        )
        copies[-1].start()
    own = pltpu.make_async_copy(mat.at[me], mat_out.at[me], own_sem)
    own.start()

    def finish(cols, total):
        depth[:, cols] = total

    sum_groups(by_z, by_x, finish, *scratch)
    own.wait()
    for c in copies:
        c.wait()


def middle(mat, by_z, by_x):
    dma = pltpu.SemaphoreType.DMA
    return pl.pallas_call(
        middle_kernel,
        out_shape=(
            jax.ShapeDtypeStruct((NP, CAP, TS, TS), BF16),
            jax.ShapeDtypeStruct((ROWS, WIN), F32),
        ),
        in_specs=[ANY, VMEM, VMEM],
        out_specs=(ANY, VMEM),
        scratch_shapes=[dma(()), dma((NP,)), dma((NP,))] + sum_scratch(),
        compiler_params=pltpu.CompilerParams(
            collective_id=1, has_side_effects=True, vmem_limit_bytes=40 * 2**20
        ),
        name="sum_depth",
    )(mat.reshape(NP, CAP, TS, TS), by_z, by_x)


def last_kernel(by_z, by_x, depth, coadd, *scratch):
    number = greet_groups()
    pl.semaphore_wait(pltpu.get_barrier_semaphore(), number)

    def finish(cols, total):
        coadd[:, cols] = total / jnp.maximum(depth[:, cols], 1.0)

    sum_groups(by_z, by_x, finish, *scratch)


def last(by_z, by_x, depth):
    return pl.pallas_call(
        last_kernel,
        out_shape=jax.ShapeDtypeStruct((ROWS, WIN), F32),
        in_specs=[VMEM, VMEM, VMEM],
        out_specs=VMEM,
        scratch_shapes=sum_scratch(),
        compiler_params=pltpu.CompilerParams(
            collective_id=2, has_side_effects=True, vmem_limit_bytes=40 * 2**20
        ),
        name="sum_numerator",
    )(by_z, by_x, depth)


def local(images, variances, bad_pixels, routes, offsets, tile_visits, coefficients, kernel_counts, taps):
    reach = taps.shape[2] // 2
    active = (lax.iota(jnp.int32, NB)[None, :] < kernel_counts[:, None])[:, None, :]
    coefs = jnp.where(active, coefficients.astype(F32), 0.0).reshape(-1)
    wide = taps.astype(F32)
    gap = jnp.zeros((NB, 2 * TS - taps.shape[2]), F32)
    vertical, horizontal = wide[:, 0], wide[:, 1, ::-1]
    rolls = jnp.concatenate(
        [jnp.concatenate([r[:, reach:], gap, r[:, :reach]], axis=1) for r in (vertical, horizontal)], axis=0
    )
    target = routes[:, 0]
    order = lax.iota(jnp.int32, NT)
    same = (target[:, None] == target[None, :]) & (order[None, :] < order[:, None])
    slot = target * CAP + jnp.sum(same.astype(jnp.int32), axis=1)
    chosen = slot[None, :] == lax.iota(jnp.int32, NP * CAP)[:, None]
    facts = jnp.stack([8 * offsets[:, 0], 8 * offsets[:, 1], jnp.ones_like(order), order], axis=0)
    slot_facts = jnp.sum(jnp.where(chosen[None], facts[:, None, :], 0), axis=2)
    table = jnp.concatenate([slot_facts[3], offsets.reshape(-1), tile_visits])
    meta = jnp.pad(slot_facts[:3].T, ((0, 0), (0, TS - 3))).reshape(NP, CAP, TS)

    wgt, mat, meta = front(table, coefs, rolls, meta, images, variances, bad_pixels)
    meta = meta.reshape(NP * CAP, TS)
    mat, depth = middle(mat, *add_tiles(meta, wgt))
    coadd = last(*add_tiles(meta, wgt, mat), depth)
    return coadd, depth


def solution(mesh):
    tiles = P(("patch", "visit"), None, None)
    return jax.shard_map(
        local,
        mesh=mesh,
        in_specs=(
            tiles, tiles, tiles,
            P(("patch", "visit"), None), P(("patch", "visit"), None), P(("patch", "visit")),
            P("visit", None, None), P("visit"), P(),
        ),
        out_specs=(P(("patch", "visit"), None), P(("patch", "visit"), None)),
        check_vma=False,
    )
```

```python
import jax
import jax.numpy as jnp
from jax import lax
from jax.experimental import pallas as pl
from jax.experimental.pallas import tpu as pltpu
from jax.sharding import PartitionSpec as P

TS = 128
WIN = 1024
CAP = 8
NB = 16
NT = 32
NP = 8
NA = 4
NZ = 8
SIDE = 16
STEPS = ((2, 0), (2, 1), (1, 0), (3, 0), (1, 1), (3, 1), (0, 1), (0, 0))
BLOCKS = (4, 3, 5, 2, 6, 1, 7, 0)
PIECES = (slice(0, 1), slice(1, 3), slice(3, 5), slice(5, 7), slice(7, 8))
FAR_PIECES = (slice(0, 3), slice(3, 8))
MESH = pl.DeviceIdType.MESH
BF16 = jnp.bfloat16
F32 = jnp.float32
VMEM = pl.BlockSpec(memory_space=pltpu.VMEM)
SMEM = pl.BlockSpec(memory_space=pltpu.SMEM)
HBM = pl.BlockSpec(memory_space=pltpu.HBM)
ANY = pl.BlockSpec(memory_space=pl.ANY)


def place():
    patch, visit = lax.axis_index("patch"), lax.axis_index("visit")
    return visit // NZ, patch // 2, lax.rem(visit, NZ), lax.rem(patch, 2)


def patch_at(ring, core, step):
    return lax.rem(ring + step[0], NA) * 2 + lax.rem(core + step[1], 2)


def signal(device):
    pl.semaphore_signal(pltpu.get_barrier_semaphore(), inc=1, device_id=device, device_id_type=MESH)


def wait(number):
    pl.semaphore_wait(pltpu.get_barrier_semaphore(), number)


def send(src, dst, send_sem, recv_sem, device):
    copy = pltpu.make_async_remote_copy(
        src_ref=src, dst_ref=dst, send_sem=send_sem, recv_sem=recv_sem, device_id=device, device_id_type=MESH
    )
    copy.start()
    return copy


def slot_kernel(routes, offsets, table, meta, count, first):
    _, y, _, core = place()
    lane = lax.broadcasted_iota(jnp.int32, (1, TS), 1)
    meta[...] = jnp.zeros_like(meta)
    for j in range(NP * CAP):
        table[j] = 0
    for p in range(NP):
        count[p] = 0

    def tally(t, carry):
        p = routes[0, t]
        count[p] = count[p] + 1
        return carry

    lax.fori_loop(0, NT, tally, 0)
    begin = 0
    for step in STEPS:
        p = patch_at(y, core, step)
        first[p] = begin
        begin = begin + count[p]
        count[p] = 0

    def fill(t, carry):
        p = routes[0, t]
        s = count[p]
        count[p] = s + 1
        i = first[p] + s
        table[NP * CAP + i] = t
        table[p * CAP + s] = i
        facts = jnp.where(lane == 1, 8 * offsets[1, t], jnp.where(lane == 2, 1, 0))
        meta[p, pl.ds(s, 1), :] = jnp.where(lane == 0, 8 * offsets[0, t], facts)
        return carry

    lax.fori_loop(0, NT, fill, 0)


def slots(routes, offsets):
    return pl.pallas_call(
        slot_kernel,
        out_shape=(
            jax.ShapeDtypeStruct((NP * CAP + NT,), jnp.int32),
            jax.ShapeDtypeStruct((NP, CAP, TS), jnp.int32),
        ),
        in_specs=[SMEM, SMEM],
        out_specs=(SMEM, VMEM),
        scratch_shapes=[pltpu.SMEM((NP,), jnp.int32), pltpu.SMEM((NP,), jnp.int32)],
        name="slots",
    )(routes, offsets)


def band(row):
    wide = jnp.broadcast_to(row, (TS, 2 * TS))
    return pltpu.roll(wide, 0, 1, stride=1, stride_axis=0)[:, :TS].astype(BF16)


def match_kernel(
    table, offsets, visits, counts, coefs, taps, meta, img_in, var_in, bad_in, wgt_out, num_out, facts_out,
    img, var, bad, weights, products, wslots, nslots, vert, horz, lm, rows, in_sem, own_sem, send_sem, recv_sem,
):
    x, y, z, core = place()
    loads = [
        pltpu.make_async_copy(src, dst, in_sem.at[i])
        for i, (src, dst) in enumerate(((var_in, var), (bad_in, bad), (img_in, img)))
    ]
    for load in loads:
        load.start()

    def along_x(step):
        return {"patch": y * 2 + lax.rem(core + step[1], 2), "visit": lax.rem(x + step[0], NA) * NZ + z}

    def along_y(step):
        return {"patch": patch_at(y, core, step)}

    for step in STEPS[:-1]:
        signal(along_x(step))
        signal(along_y(step))

    loads[0].wait()
    loads[1].wait()

    def weigh(i, carry):
        t = table[NP * CAP + i]
        weights[i] = jnp.where(bad[t] == 0, 1.0 / var[t].astype(F32), 0.0).astype(BF16)
        return carry

    lax.fori_loop(0, NT, weigh, 0)
    copies = []

    def to_patch(kind, r):
        source, made, out = ((weights, wslots, wgt_out), (products, nslots, num_out))[kind]
        ring = x if kind == 0 else y
        there, here = patch_at(ring, core, STEPS[r]), ring * 2 + core

        def sort(j, carry):
            made[j] = source[table[j]]
            return carry

        lax.fori_loop(there * CAP, there * CAP + CAP, sort, 0)
        pairs = ((meta.at[there], facts_out.at[kind, here]), (made.at[pl.ds(there * CAP, CAP)], out.at[here]))
        for i, (src, dst) in enumerate(pairs):
            if r == NP - 1:
                copy = pltpu.make_async_copy(src, dst, own_sem.at[kind, i])
                copy.start()
            else:
                device = along_x(STEPS[r]) if kind == 0 else along_y(STEPS[r])
                copy = send(src, dst, send_sem.at[kind, i, r], recv_sem.at[kind, i, r], device)
            copies.append(copy)

    wait(2 * (NP - 1))
    for r in range(NP):
        to_patch(0, r)

    span = taps.shape[2]
    tap = lax.broadcasted_iota(jnp.int32, (span, 2 * TS), 0) - span // 2
    spot = lax.broadcasted_iota(jnp.int32, (span, 2 * TS), 1)
    spot = jnp.where(spot < TS, spot, spot - 2 * TS)
    down = jnp.dot(taps[:, 0, :], (spot == tap).astype(BF16), preferred_element_type=F32)
    across = jnp.dot(taps[:, 1, :], (spot == -tap).astype(BF16), preferred_element_type=F32)
    horz[...] = jnp.zeros_like(horz)
    for k in range(NB):
        vert[k * TS : (k + 1) * TS, :] = band(down[k : k + 1, :])
        half = slice((k % 2) * TS, (k % 2 + 1) * TS)
        horz[k // 2, half, half] = band(across[k : k + 1, :])
    level = lax.broadcasted_iota(jnp.int32, (NB, NB), 0)
    column = lax.broadcasted_iota(jnp.int32, (NB, NB), 1)
    for v in range(2):
        for c in range(3):
            used = (level == column) & (level < counts[v])
            diagonal = jnp.where(used, coefs[c, v : v + 1, :].astype(F32), 0.0).astype(BF16)
            rows[v, c] = jnp.dot(diagonal, jnp.ones((NB, TS), BF16), preferred_element_type=F32)
    loads[2].wait()

    row_iota = lax.broadcasted_iota(jnp.int32, (TS, TS), 0)
    col_iota = lax.broadcasted_iota(jnp.int32, (1, TS), 1)

    def pair(step, carry):
        ids = [table[NP * CAP + 2 * step + i] for i in range(2)]
        two = jnp.concatenate([img[ids[0]], img[ids[1]]], axis=1)
        own_visit = [visits[t] for t in ids]
        rho = [(row_iota + 8 * offsets[0, t]).astype(F32) * (1.0 / WIN) for t in ids]
        gamma = [(col_iota + 8 * offsets[1, t]).astype(F32) * (1.0 / WIN) for t in ids]
        for part in range(NB // 4):
            blurred = jnp.dot(
                vert[part * 4 * TS : (part + 1) * 4 * TS, :], two, preferred_element_type=F32
            )
            for kk in range(4):
                k = part * 4 + kk
                for i in range(2):
                    lm[i * TS : (i + 1) * TS, k * TS : (k + 1) * TS] = blurred[
                        kk * TS : (kk + 1) * TS, i * TS : (i + 1) * TS
                    ].astype(BF16)
        matched = [None, None]
        for kp in range(NB // 2):
            smooth = jnp.dot(lm[:, kp * 2 * TS : (kp + 1) * 2 * TS], horz[kp], preferred_element_type=F32)
            for kk in range(2):
                k = 2 * kp + kk
                for i in range(2):
                    a0, a1, a2 = (rows[own_visit[i], c, k : k + 1, :] for c in range(3))
                    term = (a1 * rho[i] + (a0 + a2 * gamma[i])) * smooth[
                        i * TS : (i + 1) * TS, kk * TS : (kk + 1) * TS
                    ]
                    matched[i] = term if matched[i] is None else matched[i] + term
        for i in range(2):
            weight = weights[2 * step + i].astype(F32)
            products[2 * step + i] = (weight * matched[i].astype(BF16).astype(F32)).astype(BF16)
        return carry

    for r in range(NT // CAP):
        lax.fori_loop(r * CAP // 2, (r + 1) * CAP // 2, pair, 0)
        if r < NT // CAP - 1:
            to_patch(1, r)
    for r in range(NT // CAP - 1, NP):
        to_patch(1, r)
    for copy in copies:
        copy.wait()


def match(*operands):
    dma = pltpu.SemaphoreType.DMA
    got = jax.ShapeDtypeStruct((NP, CAP, TS, TS), BF16)
    facts = jax.ShapeDtypeStruct((2, NP, CAP, TS), jnp.int32)
    return pl.pallas_call(
        match_kernel,
        out_shape=(got, got, facts),
        in_specs=[SMEM, SMEM, SMEM, SMEM, VMEM, VMEM, VMEM, HBM, HBM, HBM],
        out_specs=(ANY, ANY, ANY),
        scratch_shapes=[
            pltpu.VMEM((NT, TS, TS), BF16),
            pltpu.VMEM((NT, TS, TS), BF16),
            pltpu.VMEM((NT, TS, TS), jnp.int32),
            pltpu.VMEM((NT, TS, TS), BF16),
            pltpu.VMEM((NT, TS, TS), BF16),
            pltpu.VMEM((NP * CAP, TS, TS), BF16),
            pltpu.VMEM((NP * CAP, TS, TS), BF16),
            pltpu.VMEM((NB * TS, TS), BF16),
            pltpu.VMEM((NB // 2, 2 * TS, 2 * TS), BF16),
            pltpu.VMEM((2 * TS, NB * TS), BF16),
            pltpu.VMEM((2, 3, NB, TS), F32),
            dma((3,)), dma((2, 2)), dma((2, 2, NP)), dma((2, 2, NP)),
        ],
        compiler_params=pltpu.CompilerParams(
            collective_id=0, has_side_effects=True, vmem_limit_bytes=54 * 2**20
        ),
        name="match_tiles",
    )(*operands)


def add_kernel(facts, wgt, num, wgt_sum, num_sum, wgt_window, num_window):
    source = pl.program_id(0)
    planes = ((0, wgt, wgt_sum, wgt_window), (1, num, num_sum, num_window))

    @pl.when(source == 0)
    def _():
        def clear(i, carry):
            for plane in planes:
                plane[3][i] = jnp.zeros((WIN, TS), F32)
            return carry

        lax.fori_loop(0, WIN // TS + 1, clear, 0)

    lane = lax.broadcasted_iota(jnp.int32, (TS, TS), 1)
    for kind, tiles, _, window in planes:
        work = []
        for s in range(CAP):
            j = source * CAP + s
            used = facts[kind, j, 2]
            top = pl.multiple_of(facts[kind, j, 0], 8)
            left = facts[kind, j, 1]
            shift = lax.rem(left, TS)
            tile = pltpu.roll(tiles[s].astype(F32), shift, 1)
            here = lane >= jnp.where(used > 0, shift, TS)
            there = lane < jnp.where(used > 0, shift, 0)
            work.append((left // TS, top, tile, here, there))
        for q, top, tile, here, there in work:
            window[q, pl.ds(top, TS), :] += jnp.where(here, tile, 0.0)
            window[q + 1, pl.ds(top, TS), :] += jnp.where(there, tile, 0.0)

    @pl.when(source == NP - 1)
    def _():
        _, _, z, _ = place()

        def write(a, carry):
            for i, k in enumerate(BLOCKS):
                v = a * NZ + lax.rem(z + k, NZ)
                for half in range(2):
                    at = pl.multiple_of((2 * v + half) * SIDE, SIDE)
                    for _, _, out, window in planes:
                        for q in range(WIN // TS):
                            out[a, i, half, :, q * TS : (q + 1) * TS] = window[q, pl.ds(at, SIDE), :].astype(BF16)
            return carry

        lax.fori_loop(0, NA, write, 0)


def add_tiles(wgt, num, facts):
    block = pl.BlockSpec((CAP, TS, TS), lambda i: (i, 0, 0))
    out = jax.ShapeDtypeStruct((NA, NZ, 2, SIDE, WIN), BF16)
    tiles = [t.reshape(NP * CAP, TS, TS) for t in (wgt, num)]
    return pl.pallas_call(
        add_kernel,
        grid=(NP,),
        out_shape=(out, out),
        in_specs=[SMEM, block, block],
        out_specs=(VMEM, VMEM),
        scratch_shapes=[pltpu.VMEM((WIN // TS + 1, WIN, TS), F32)] * 2,
        compiler_params=pltpu.CompilerParams(vmem_limit_bytes=40 * 2**20),
        name="add_tiles",
    )(facts.reshape(2, NP * CAP, TS), *tiles)


class Plane:
    def __init__(self, a, z, along_a, along_z, src, a_recv, a_send, mid, z_recv, z_send, as_sem, ar_sem, zs_sem, zr_sem):
        self.a, self.z, self.along_a, self.along_z, self.src = a, z, along_a, along_z, src
        self.a_recv, self.a_send, self.mid, self.z_recv, self.z_send = a_recv, a_send, mid, z_recv, z_send
        self.as_sem, self.ar_sem, self.zs_sem, self.zr_sem = as_sem, ar_sem, zs_sem, zr_sem
        self.copies = {}

    def pass_on(self, name, way, step, i, src, dst):
        to = self.along_a(lax.rem(self.a + (1, NA - 1)[way], NA))
        sems = self.as_sem.at[way, step, i], self.ar_sem.at[way, step, i]
        self.copies[name, way, i] = send(src, dst, *sems, to)

    def first(self, i):
        piece = FAR_PIECES[i]
        for way in range(2):
            there = self.src.at[lax.rem(self.a + 2, NA), piece, way]
            self.pass_on("far", way, 0, i, there, self.a_recv.at[way, 0, piece])

    def second(self, i):
        piece = PIECES[i]
        for f, far in enumerate(FAR_PIECES):
            if far.start == piece.start:
                for way in range(2):
                    self.copies["far", way, f].wait_recv()
        for way in range(2):
            to = lax.rem(self.a + (1, NA - 1)[way], NA)
            mine = self.src[to, piece, way].astype(F32)
            self.a_send[way, piece] = (mine + self.a_recv[way, 0, piece].astype(F32)).astype(BF16)
            self.pass_on("sum", way, 2, i, self.a_send.at[way, piece], self.a_recv.at[way, 2, piece])
            self.pass_on("raw", way, 1, i, self.src.at[to, piece, 1 - way], self.a_recv.at[way, 1, piece])

    def ready(self, i):
        for way in range(2):
            self.copies["raw", way, i].wait_recv()
            self.copies["sum", way, i].wait_recv()

    def ring_sum(self, at):
        return [
            self.src[self.a, at, half].astype(F32)
            + self.a_recv[half, 2, at].astype(F32)
            + self.a_recv[1 - half, 1, at].astype(F32)
            for half in range(2)
        ]

    def keep(self, at):
        for half, value in enumerate(self.ring_sum(at)):
            self.mid[at, half] = value.astype(BF16)

    def along(self, j):
        for way in range(2):
            at = BLOCKS.index(4 - j if way == 0 else 4 + j)
            to = self.along_z(lax.rem(self.z + (1 if way == 0 else NZ - 1), NZ))
            if j == 0:
                src, dst = self.mid.at[at, way], self.z_recv.at[way, 0, way]
            else:
                src, dst = self.z_send.at[way, j - 1], self.z_recv.at[way, j]
                self.copies["z", way, j - 1].wait_recv()
                block, got = self.mid.at[at], self.z_recv.at[way, j - 1]
                src[way] = (block[way].astype(F32) + got[way].astype(F32)).astype(BF16)
                if j == 1:
                    src[1 - way] = block[1 - way]
                else:
                    src[1 - way] = (block[1 - way].astype(F32) + got[1 - way].astype(F32)).astype(BF16)
            self.copies["z", way, j] = send(src, dst, self.zs_sem.at[way, j], self.zr_sem.at[way, j], to)

    def total(self):
        out = self.ring_sum(NZ - 1)
        for way in range(2):
            self.copies["z", way, 3].wait_recv()
            out = [value + self.z_recv[way, 3, half].astype(F32) for half, value in enumerate(out)]
        return jnp.concatenate(out, axis=0)

    def finish(self):
        for copy in self.copies.values():
            copy.wait_send()


PLANE_SCRATCH = 9


def plane_scratch():
    block = (2, SIDE, WIN)
    dma = pltpu.SemaphoreType.DMA
    return [
        pltpu.VMEM((2, 3, NZ, SIDE, WIN), BF16),
        pltpu.VMEM((2, NZ, SIDE, WIN), BF16),
        pltpu.VMEM((NZ,) + block, BF16),
        pltpu.VMEM((2, NZ // 2) + block, BF16),
        pltpu.VMEM((2, NZ // 2 - 1) + block, BF16),
        dma((2, 3, len(PIECES))), dma((2, 3, len(PIECES))), dma((2, NZ // 2)), dma((2, NZ // 2)),
    ]


def sum_kernel(wgt, num, coadd, depth, *scratch):
    x, y, z, core = place()
    along_x = lambda to: {"visit": to * NZ + z}
    along_y = lambda to: {"patch": to * 2 + core}
    along_z = lambda to: {"visit": x * NZ + to}
    swapped = {"patch": x * 2 + core, "visit": y * NZ + z}
    moved, swap_send, swap_recv = scratch[2 * PLANE_SCRATCH :]

    for to in (1, NA - 1):
        signal(along_x(lax.rem(x + to, NA)))
        signal(along_y(lax.rem(y + to, NA)))
    for to in (1, NZ - 1):
        signal(along_z(lax.rem(z + to, NZ)))

    @pl.when(x != y)
    def _():
        signal(swapped)
        wait(7)

    @pl.when(x == y)
    def _():
        wait(6)

    planes = (
        Plane(y, z, along_y, along_z, wgt, *scratch[:PLANE_SCRATCH]),
        Plane(x, z, along_x, along_z, num, *scratch[PLANE_SCRATCH : 2 * PLANE_SCRATCH]),
    )
    for i in range(len(FAR_PIECES)):
        for plane in planes:
            plane.first(i)
    for i in range(len(PIECES)):
        for plane in planes:
            plane.second(i)
    for i in range(len(PIECES)):
        for plane in planes:
            plane.ready(i)
            for at in range(NZ - 1)[PIECES[i]]:
                plane.keep(at)
        if i < NZ // 2:
            for plane in planes:
                plane.along(i)
    total = planes[0].total()

    @pl.when(x != y)
    def _():
        moved[...] = total
        send(moved, depth, swap_send, swap_recv, swapped).wait()

    @pl.when(x == y)
    def _():
        depth[...] = total

    coadd[...] = planes[1].total() / jnp.maximum(depth[...], 1.0)
    for plane in planes:
        plane.finish()


def sum_windows(wgt, num):
    out = jax.ShapeDtypeStruct((2 * SIDE, WIN), F32)
    return pl.pallas_call(
        sum_kernel,
        out_shape=(out, out),
        in_specs=[VMEM, VMEM],
        out_specs=(VMEM, VMEM),
        scratch_shapes=plane_scratch()
        + plane_scratch()
        + [pltpu.VMEM((2 * SIDE, WIN), F32), pltpu.SemaphoreType.DMA, pltpu.SemaphoreType.DMA],
        compiler_params=pltpu.CompilerParams(
            collective_id=1, has_side_effects=True, vmem_limit_bytes=40 * 2**20
        ),
        name="sum_windows",
    )(wgt, num)


def local(images, variances, bad_pixels, routes, offsets, tile_visits, coefficients, kernel_counts, taps):
    routes, offsets, coefficients = routes.T, offsets.T, coefficients.transpose(1, 0, 2)
    table, meta = slots(routes, offsets)
    got = match(
        table, offsets, tile_visits, kernel_counts, coefficients, taps, meta, images, variances, bad_pixels
    )
    return sum_windows(*add_tiles(*got))


def solution(mesh):
    tiles = P(("patch", "visit"), None, None)
    return jax.shard_map(
        local,
        mesh=mesh,
        in_specs=(
            tiles, tiles, tiles,
            P(("patch", "visit"), None), P(("patch", "visit"), None), P(("patch", "visit")),
            P("visit", None, None), P("visit"), P(),
        ),
        out_specs=(P(("patch", "visit"), None), P(("patch", "visit"), None)),
        check_vma=False,
    )
```

```python
import jax
import jax.numpy as jnp
from jax import lax
from jax.experimental import pallas as pl
from jax.experimental.pallas import tpu as pltpu
from jax.sharding import PartitionSpec as P

TS = 128
WIN = 1024
CAP = 8
NB = 16
NT = 32
NP = 8
NA = 4
NZ = 8
SIDE = 16
STEPS = ((2, 0), (2, 1), (1, 0), (3, 0), (1, 1), (3, 1), (0, 1), (0, 0))
BLOCKS = (4, 3, 5, 2, 6, 1, 7, 0)
PIECES = (slice(0, 1), slice(1, 3), slice(3, 5), slice(5, 7), slice(7, 8))
FAR_PIECES = (slice(0, 3), slice(3, 8))
MESH = pl.DeviceIdType.MESH
BF16 = jnp.bfloat16
F32 = jnp.float32
VMEM = pl.BlockSpec(memory_space=pltpu.VMEM)
SMEM = pl.BlockSpec(memory_space=pltpu.SMEM)
HBM = pl.BlockSpec(memory_space=pltpu.HBM)
ANY = pl.BlockSpec(memory_space=pl.ANY)


def place():
    patch, visit = lax.axis_index("patch"), lax.axis_index("visit")
    return visit // NZ, patch // 2, lax.rem(visit, NZ), lax.rem(patch, 2)


def patch_at(ring, core, step):
    return lax.rem(ring + step[0], NA) * 2 + lax.rem(core + step[1], 2)


def signal(device):
    pl.semaphore_signal(pltpu.get_barrier_semaphore(), inc=1, device_id=device, device_id_type=MESH)


def wait(number):
    pl.semaphore_wait(pltpu.get_barrier_semaphore(), number)


def send(src, dst, send_sem, recv_sem, device):
    copy = pltpu.make_async_remote_copy(
        src_ref=src, dst_ref=dst, send_sem=send_sem, recv_sem=recv_sem, device_id=device, device_id_type=MESH
    )
    copy.start()
    return copy


def slot_kernel(routes, offsets, table, meta, count, first):
    _, y, _, core = place()
    lane = lax.broadcasted_iota(jnp.int32, (1, TS), 1)
    meta[...] = jnp.zeros_like(meta)
    for j in range(NP * CAP):
        table[j] = 0
    for p in range(NP):
        count[p] = 0

    def tally(t, carry):
        p = routes[0, t]
        count[p] = count[p] + 1
        return carry

    lax.fori_loop(0, NT, tally, 0)
    begin = 0
    for step in STEPS:
        p = patch_at(y, core, step)
        first[p] = begin
        begin = begin + count[p]
        count[p] = 0

    def fill(t, carry):
        p = routes[0, t]
        s = count[p]
        count[p] = s + 1
        i = first[p] + s
        table[NP * CAP + i] = t
        table[p * CAP + s] = i
        facts = jnp.where(lane == 1, 8 * offsets[1, t], jnp.where(lane == 2, 1, 0))
        meta[p, pl.ds(s, 1), :] = jnp.where(lane == 0, 8 * offsets[0, t], facts)
        return carry

    lax.fori_loop(0, NT, fill, 0)


def slots(routes, offsets):
    return pl.pallas_call(
        slot_kernel,
        out_shape=(
            jax.ShapeDtypeStruct((NP * CAP + NT,), jnp.int32),
            jax.ShapeDtypeStruct((NP, CAP, TS), jnp.int32),
        ),
        in_specs=[SMEM, SMEM],
        out_specs=(SMEM, VMEM),
        scratch_shapes=[pltpu.SMEM((NP,), jnp.int32), pltpu.SMEM((NP,), jnp.int32)],
        name="slots",
    )(routes, offsets)


def band(row):
    wide = jnp.broadcast_to(row, (TS, 2 * TS))
    return pltpu.roll(wide, 0, 1, stride=1, stride_axis=0)[:, :TS].astype(BF16)


def match_kernel(
    table, offsets, visits, counts, coefs, taps, meta, img_in, var_in, bad_in, wgt_out, num_out, facts_out,
    img, var, bad, weights, products, wslots, nslots, vert, horz, lm, rows, in_sem, own_sem, send_sem, recv_sem,
):
    x, y, z, core = place()
    loads = [
        pltpu.make_async_copy(src, dst, in_sem.at[i])
        for i, (src, dst) in enumerate(((var_in, var), (bad_in, bad), (img_in, img)))
    ]
    for load in loads:
        load.start()

    def along_x(step):
        return {"patch": y * 2 + lax.rem(core + step[1], 2), "visit": lax.rem(x + step[0], NA) * NZ + z}

    def along_y(step):
        return {"patch": patch_at(y, core, step)}

    for step in STEPS[:-1]:
        signal(along_x(step))
        signal(along_y(step))

    span = taps.shape[2]
    tap = lax.broadcasted_iota(jnp.int32, (span, 2 * TS), 0) - span // 2
    spot = lax.broadcasted_iota(jnp.int32, (span, 2 * TS), 1)
    spot = jnp.where(spot < TS, spot, spot - 2 * TS)
    down = jnp.dot(taps[:, 0, :], (spot == tap).astype(BF16), preferred_element_type=F32)
    across = jnp.dot(taps[:, 1, :], (spot == -tap).astype(BF16), preferred_element_type=F32)
    horz[...] = jnp.zeros_like(horz)
    for k in range(NB):
        vert[k * TS : (k + 1) * TS, :] = band(down[k : k + 1, :])
        half = slice((k % 2) * TS, (k % 2 + 1) * TS)
        horz[k // 2, half, half] = band(across[k : k + 1, :])
    level = lax.broadcasted_iota(jnp.int32, (NB, NB), 0)
    column = lax.broadcasted_iota(jnp.int32, (NB, NB), 1)
    for v in range(2):
        for c in range(3):
            used = (level == column) & (level < counts[v])
            diagonal = jnp.where(used, coefs[c, v : v + 1, :].astype(F32), 0.0).astype(BF16)
            rows[v, c] = jnp.dot(diagonal, jnp.ones((NB, TS), BF16), preferred_element_type=F32)
    loads[0].wait()
    loads[1].wait()

    def weigh(i, carry):
        t = table[NP * CAP + i]
        weights[i] = jnp.where(bad[t] == 0, 1.0 / var[t].astype(F32), 0.0).astype(BF16)
        return carry

    copies = []

    def to_patch(kind, r, begin=0, end=CAP):
        source, made, out = ((weights, wslots, wgt_out), (products, nslots, num_out))[kind]
        ring = x if kind == 0 else y
        there, here = patch_at(ring, core, STEPS[r]), ring * 2 + core

        def sort(j, carry):
            made[j] = source[table[j]]
            return carry

        lax.fori_loop(there * CAP + begin, there * CAP + end, sort, 0)
        tiles = made.at[pl.ds(there * CAP + begin, end - begin)], out.at[here, pl.ds(begin, end - begin)]
        pairs = [(0 if end == CAP else 1, *tiles)]
        if end == CAP:
            pairs.append((2, meta.at[there], facts_out.at[kind, here]))
        for i, src, dst in pairs:
            if r == NP - 1:
                copy = pltpu.make_async_copy(src, dst, own_sem.at[kind, i])
                copy.start()
            else:
                device = along_x(STEPS[r]) if kind == 0 else along_y(STEPS[r])
                copy = send(src, dst, send_sem.at[kind, i, r], recv_sem.at[kind, i, r], device)
            copies.append(copy)

    lax.fori_loop(0, CAP // 2, weigh, 0)
    loads[2].wait()

    row_iota = lax.broadcasted_iota(jnp.int32, (TS, TS), 0)
    col_iota = lax.broadcasted_iota(jnp.int32, (1, TS), 1)

    def pair(step, carry):
        ids = [table[NP * CAP + 2 * step + i] for i in range(2)]
        two = jnp.concatenate([img[ids[0]], img[ids[1]]], axis=1)
        own_visit = [visits[t] for t in ids]
        rho = [(row_iota + 8 * offsets[0, t]).astype(F32) * (1.0 / WIN) for t in ids]
        gamma = [(col_iota + 8 * offsets[1, t]).astype(F32) * (1.0 / WIN) for t in ids]
        for part in range(NB // 4):
            blurred = jnp.dot(
                vert[part * 4 * TS : (part + 1) * 4 * TS, :], two, preferred_element_type=F32
            )
            for kk in range(4):
                k = part * 4 + kk
                for i in range(2):
                    lm[i * TS : (i + 1) * TS, k * TS : (k + 1) * TS] = blurred[
                        kk * TS : (kk + 1) * TS, i * TS : (i + 1) * TS
                    ].astype(BF16)
        matched = [None, None]
        for kp in range(NB // 2):
            smooth = jnp.dot(lm[:, kp * 2 * TS : (kp + 1) * 2 * TS], horz[kp], preferred_element_type=F32)
            for kk in range(2):
                k = 2 * kp + kk
                for i in range(2):
                    a0, a1, a2 = (rows[own_visit[i], c, k : k + 1, :] for c in range(3))
                    term = (a1 * rho[i] + (a0 + a2 * gamma[i])) * smooth[
                        i * TS : (i + 1) * TS, kk * TS : (kk + 1) * TS
                    ]
                    matched[i] = term if matched[i] is None else matched[i] + term
        for i in range(2):
            weight = weights[2 * step + i].astype(F32)
            products[2 * step + i] = (weight * matched[i].astype(BF16).astype(F32)).astype(BF16)
        return carry

    lax.fori_loop(0, CAP // 4, pair, 0)
    wait(2 * (NP - 1))
    to_patch(1, 0, 0, CAP // 2)
    lax.fori_loop(CAP // 2, NT, weigh, 0)
    for r in range(2):
        to_patch(0, r)
    lax.fori_loop(CAP // 4, CAP // 2, pair, 0)
    to_patch(1, 0, CAP // 2)
    for r in range(2, NP):
        to_patch(0, r)
    for r in range(1, NT // CAP):
        lax.fori_loop(r * CAP // 2, (r + 1) * CAP // 2, pair, 0)
        if r < NT // CAP - 1:
            to_patch(1, r)
    for r in range(NT // CAP - 1, NP):
        to_patch(1, r)
    for copy in copies:
        copy.wait()


def match(*operands):
    dma = pltpu.SemaphoreType.DMA
    got = jax.ShapeDtypeStruct((NP, CAP, TS, TS), BF16)
    facts = jax.ShapeDtypeStruct((2, NP, CAP, TS), jnp.int32)
    return pl.pallas_call(
        match_kernel,
        out_shape=(got, got, facts),
        in_specs=[SMEM, SMEM, SMEM, SMEM, VMEM, VMEM, VMEM, HBM, HBM, HBM],
        out_specs=(ANY, ANY, ANY),
        scratch_shapes=[
            pltpu.VMEM((NT, TS, TS), BF16),
            pltpu.VMEM((NT, TS, TS), BF16),
            pltpu.VMEM((NT, TS, TS), jnp.int32),
            pltpu.VMEM((NT, TS, TS), BF16),
            pltpu.VMEM((NT, TS, TS), BF16),
            pltpu.VMEM((NP * CAP, TS, TS), BF16),
            pltpu.VMEM((NP * CAP, TS, TS), BF16),
            pltpu.VMEM((NB * TS, TS), BF16),
            pltpu.VMEM((NB // 2, 2 * TS, 2 * TS), BF16),
            pltpu.VMEM((2 * TS, NB * TS), BF16),
            pltpu.VMEM((2, 3, NB, TS), F32),
            dma((3,)), dma((2, 3)), dma((2, 3, NP)), dma((2, 3, NP)),
        ],
        compiler_params=pltpu.CompilerParams(
            collective_id=0, has_side_effects=True, vmem_limit_bytes=54 * 2**20
        ),
        name="match_tiles",
    )(*operands)


def add_kernel(facts, wgt, num, wgt_sum, num_sum, wgt_window, num_window, wgt_tiles, num_tiles, sem):
    planes = ((0, wgt_tiles, wgt_sum, wgt_window), (1, num_tiles, num_sum, num_window))

    def loads(source):
        part = pl.ds(pl.multiple_of(source * CAP, CAP), CAP)
        return (
            pltpu.make_async_copy(wgt.at[part], wgt_tiles.at[part], sem.at[0, source]),
            pltpu.make_async_copy(num.at[part], num_tiles.at[part], sem.at[1, source]),
        )

    for source in range(NP):
        for load in loads(source):
            load.start()

    def clear(i, carry):
        for plane in planes:
            plane[3][i] = jnp.zeros((WIN, TS), F32)
        return carry

    lax.fori_loop(0, WIN // TS + 1, clear, 0)
    lane = lax.broadcasted_iota(jnp.int32, (TS, TS), 1)

    def add(source, carry):
        arriving = loads(source)
        for kind, tiles, _, window in planes:
            arriving[kind].wait()
            work = []
            for s in range(CAP):
                j = source * CAP + s
                used = facts[kind, j, 2]
                top = pl.multiple_of(facts[kind, j, 0], 8)
                left = facts[kind, j, 1]
                shift = lax.rem(left, TS)
                tile = pltpu.roll(tiles[j].astype(F32), shift, 1)
                here = lane >= jnp.where(used > 0, shift, TS)
                there = lane < jnp.where(used > 0, shift, 0)
                work.append((left // TS, top, tile, here, there))
            for q, top, tile, here, there in work:
                window[q, pl.ds(top, TS), :] += jnp.where(here, tile, 0.0)
                window[q + 1, pl.ds(top, TS), :] += jnp.where(there, tile, 0.0)
        return carry

    lax.fori_loop(0, NP, add, 0)
    _, _, z, _ = place()

    def write(a, carry):
        for i, k in enumerate(BLOCKS):
            v = a * NZ + lax.rem(z + k, NZ)
            for half in range(2):
                at = pl.multiple_of((2 * v + half) * SIDE, SIDE)
                for _, _, out, window in planes:
                    for q in range(WIN // TS):
                        out[a, i, half, :, q * TS : (q + 1) * TS] = window[q, pl.ds(at, SIDE), :].astype(BF16)
        return carry

    lax.fori_loop(0, NA, write, 0)


def add_tiles(wgt, num, facts):
    out = jax.ShapeDtypeStruct((NA, NZ, 2, SIDE, WIN), BF16)
    tiles = [t.reshape(NP * CAP, TS, TS) for t in (wgt, num)]
    return pl.pallas_call(
        add_kernel,
        out_shape=(out, out),
        in_specs=[SMEM, ANY, ANY],
        out_specs=(VMEM, VMEM),
        scratch_shapes=[pltpu.VMEM((WIN // TS + 1, WIN, TS), F32)] * 2
        + [pltpu.VMEM((NP * CAP, TS, TS), BF16)] * 2
        + [pltpu.SemaphoreType.DMA((2, NP))],
        compiler_params=pltpu.CompilerParams(vmem_limit_bytes=48 * 2**20),
        name="add_tiles",
    )(facts.reshape(2, NP * CAP, TS), *tiles)


class Plane:
    def __init__(self, a, z, along_a, along_z, owner_z, src, a_recv, a_send, mid, z_recv, z_send, as_sem, ar_sem, zs_sem, zr_sem):
        self.a, self.z, self.along_a, self.along_z, self.owner_z, self.src = a, z, along_a, along_z, owner_z, src
        self.a_recv, self.a_send, self.mid, self.z_recv, self.z_send = a_recv, a_send, mid, z_recv, z_send
        self.as_sem, self.ar_sem, self.zs_sem, self.zr_sem = as_sem, ar_sem, zs_sem, zr_sem
        self.copies = {}

    def pass_on(self, name, way, step, i, src, dst):
        to = self.along_a(lax.rem(self.a + (1, NA - 1)[way], NA))
        sems = self.as_sem.at[way, step, i], self.ar_sem.at[way, step, i]
        self.copies[name, way, i] = send(src, dst, *sems, to)

    def first(self, i):
        piece = FAR_PIECES[i]
        for way in range(2):
            there = self.src.at[lax.rem(self.a + 2, NA), piece, way]
            self.pass_on("far", way, 0, i, there, self.a_recv.at[way, 0, piece])

    def second(self, i):
        piece = PIECES[i]
        for f, far in enumerate(FAR_PIECES):
            if far.start == piece.start:
                for way in range(2):
                    self.copies["far", way, f].wait_recv()
        for way in range(2):
            to = lax.rem(self.a + (1, NA - 1)[way], NA)
            mine = self.src[to, piece, way].astype(F32)
            self.a_send[way, piece] = (mine + self.a_recv[way, 0, piece].astype(F32)).astype(BF16)
            self.pass_on("sum", way, 2, i, self.a_send.at[way, piece], self.a_recv.at[way, 2, piece])
            self.pass_on("raw", way, 1, i, self.src.at[to, piece, 1 - way], self.a_recv.at[way, 1, piece])

    def ready(self, i):
        for way in range(2):
            self.copies["raw", way, i].wait_recv()
            self.copies["sum", way, i].wait_recv()

    def ring_sum(self, at):
        return [
            self.src[self.a, at, half].astype(F32)
            + self.a_recv[half, 2, at].astype(F32)
            + self.a_recv[1 - half, 1, at].astype(F32)
            for half in range(2)
        ]

    def keep(self, at):
        for half, value in enumerate(self.ring_sum(at)):
            self.mid[at, half] = value.astype(BF16)

    def along(self, j):
        for way in range(2):
            at = BLOCKS.index(4 - j if way == 0 else 4 + j)
            to = (self.along_z if j < 3 else self.owner_z)(lax.rem(self.z + (1 if way == 0 else NZ - 1), NZ))
            if j == 0:
                src, dst = self.mid.at[at, way], self.z_recv.at[way, 0, way]
            else:
                src, dst = self.z_send.at[way, j - 1], self.z_recv.at[way, j]
                self.copies["z", way, j - 1].wait_recv()
                block, got = self.mid.at[at], self.z_recv.at[way, j - 1]
                src[way] = (block[way].astype(F32) + got[way].astype(F32)).astype(BF16)
                if j == 1:
                    src[1 - way] = block[1 - way]
                else:
                    src[1 - way] = (block[1 - way].astype(F32) + got[1 - way].astype(F32)).astype(BF16)
            self.copies["z", way, j] = send(src, dst, self.zs_sem.at[way, j], self.zr_sem.at[way, j], to)

    def total(self, out):
        for way in range(2):
            self.copies["z", way, 3].wait_recv()
            out = [value + self.z_recv[way, 3, half].astype(F32) for half, value in enumerate(out)]
        return jnp.concatenate(out, axis=0)

    def finish(self):
        for copy in self.copies.values():
            copy.wait_send()


PLANE_SCRATCH = 9


def plane_scratch():
    block = (2, SIDE, WIN)
    dma = pltpu.SemaphoreType.DMA
    return [
        pltpu.VMEM((2, 3, NZ, SIDE, WIN), BF16),
        pltpu.VMEM((2, NZ, SIDE, WIN), BF16),
        pltpu.VMEM((NZ,) + block, BF16),
        pltpu.VMEM((2, NZ // 2) + block, BF16),
        pltpu.VMEM((2, NZ // 2 - 1) + block, BF16),
        dma((2, 3, len(PIECES))), dma((2, 3, len(PIECES))), dma((2, NZ // 2)), dma((2, NZ // 2)),
    ]


def sum_kernel(wgt, num, coadd, depth, *scratch):
    x, y, z, core = place()
    along_x = lambda to: {"visit": to * NZ + z}
    along_y = lambda to: {"patch": to * 2 + core}
    along_z = lambda to: {"visit": x * NZ + to}
    swapped = lambda to: {"patch": x * 2 + core, "visit": y * NZ + to}
    kept, swap_send, swap_recv = scratch[2 * PLANE_SCRATCH :]

    for to in (1, NA - 1):
        signal(along_x(lax.rem(x + to, NA)))
        signal(along_y(lax.rem(y + to, NA)))
    for to in (1, NZ - 1):
        signal(along_z(lax.rem(z + to, NZ)))
        signal(swapped(lax.rem(z + to, NZ)))

    @pl.when(x != y)
    def _():
        signal(swapped(z))
        wait(9)

    @pl.when(x == y)
    def _():
        wait(8)

    planes = (
        Plane(y, z, along_y, along_z, swapped, wgt, *scratch[:PLANE_SCRATCH]),
        Plane(x, z, along_x, along_z, along_z, num, *scratch[PLANE_SCRATCH : 2 * PLANE_SCRATCH]),
    )
    for i in range(len(FAR_PIECES)):
        for plane in planes:
            plane.first(i)
    for i in range(len(PIECES)):
        for plane in planes:
            plane.second(i)
    for i in range(len(PIECES)):
        for plane in planes:
            plane.ready(i)
            for at in range(NZ - 1)[PIECES[i]]:
                plane.keep(at)
        if i < NZ // 2:
            for plane in planes:
                plane.along(i)
    planes[0].keep(NZ - 1)
    own = planes[0].mid.at[NZ - 1]
    swap = pltpu.make_async_remote_copy(
        src_ref=own, dst_ref=kept, send_sem=swap_send, recv_sem=swap_recv, device_id=swapped(z), device_id_type=MESH
    )

    @pl.when(x != y)
    def _():
        swap.start()

    @pl.when(x == y)
    def _():
        kept[...] = own[...]

    mine = planes[1].total(planes[1].ring_sum(NZ - 1))

    @pl.when(x != y)
    def _():
        swap.wait()

    total = planes[0].total([kept[half].astype(F32) for half in range(2)])
    depth[...] = total
    coadd[...] = mine / jnp.maximum(total, 1.0)
    for plane in planes:
        plane.finish()


def sum_windows(wgt, num):
    out = jax.ShapeDtypeStruct((2 * SIDE, WIN), F32)
    return pl.pallas_call(
        sum_kernel,
        out_shape=(out, out),
        in_specs=[VMEM, VMEM],
        out_specs=(VMEM, VMEM),
        scratch_shapes=plane_scratch()
        + plane_scratch()
        + [pltpu.VMEM((2, SIDE, WIN), BF16), pltpu.SemaphoreType.DMA, pltpu.SemaphoreType.DMA],
        compiler_params=pltpu.CompilerParams(
            collective_id=1, has_side_effects=True, vmem_limit_bytes=40 * 2**20
        ),
        name="sum_windows",
    )(wgt, num)


def local(images, variances, bad_pixels, routes, offsets, tile_visits, coefficients, kernel_counts, taps):
    routes, offsets, coefficients = routes.T, offsets.T, coefficients.transpose(1, 0, 2)
    table, meta = slots(routes, offsets)
    got = match(
        table, offsets, tile_visits, kernel_counts, coefficients, taps, meta, images, variances, bad_pixels
    )
    return sum_windows(*add_tiles(*got))


def solution(mesh):
    tiles = P(("patch", "visit"), None, None)
    return jax.shard_map(
        local,
        mesh=mesh,
        in_specs=(
            tiles, tiles, tiles,
            P(("patch", "visit"), None), P(("patch", "visit"), None), P(("patch", "visit")),
            P("visit", None, None), P("visit"), P(),
        ),
        out_specs=(P(("patch", "visit"), None), P(("patch", "visit"), None)),
        check_vma=False,
    )
```

```python
import jax
import jax.numpy as jnp
from jax import lax
from jax.experimental import pallas as pl
from jax.experimental.pallas import tpu as pltpu
from jax.sharding import PartitionSpec as P

TS = 128
WIN = 1024
CAP = 8
NB = 16
NT = 32
NP = 8
NA = 4
NZ = 8
SIDE = 16
STEPS = ((2, 0), (2, 1), (1, 0), (3, 0), (1, 1), (3, 1), (0, 1), (0, 0))
BLOCKS = (4, 3, 5, 2, 6, 1, 7, 0)
PIECES = (slice(0, 1), slice(1, 3), slice(3, 5), slice(5, 7), slice(7, 8))
FAR_PIECES = (slice(0, 3), slice(3, 8))
MESH = pl.DeviceIdType.MESH
BF16 = jnp.bfloat16
F32 = jnp.float32
VMEM = pl.BlockSpec(memory_space=pltpu.VMEM)
SMEM = pl.BlockSpec(memory_space=pltpu.SMEM)
HBM = pl.BlockSpec(memory_space=pltpu.HBM)
ANY = pl.BlockSpec(memory_space=pl.ANY)


def place():
    patch, visit = lax.axis_index("patch"), lax.axis_index("visit")
    return visit // NZ, patch // 2, lax.rem(visit, NZ), lax.rem(patch, 2)


def patch_at(ring, core, step):
    return lax.rem(ring + step[0], NA) * 2 + lax.rem(core + step[1], 2)


def signal(device):
    pl.semaphore_signal(pltpu.get_barrier_semaphore(), inc=1, device_id=device, device_id_type=MESH)


def wait(number):
    pl.semaphore_wait(pltpu.get_barrier_semaphore(), number)


def send(src, dst, send_sem, recv_sem, device):
    copy = pltpu.make_async_remote_copy(
        src_ref=src, dst_ref=dst, send_sem=send_sem, recv_sem=recv_sem, device_id=device, device_id_type=MESH
    )
    copy.start()
    return copy


def slot_kernel(routes, offsets, table, meta, count, first):
    _, y, _, core = place()
    lane = lax.broadcasted_iota(jnp.int32, (1, TS), 1)
    meta[...] = jnp.zeros_like(meta)
    for j in range(NP * CAP):
        table[j] = 0
    for p in range(NP):
        count[p] = 0

    def tally(t, carry):
        p = routes[0, t]
        count[p] = count[p] + 1
        return carry

    lax.fori_loop(0, NT, tally, 0)
    begin = 0
    for step in STEPS:
        p = patch_at(y, core, step)
        first[p] = begin
        begin = begin + count[p]
        count[p] = 0

    def fill(t, carry):
        p = routes[0, t]
        s = count[p]
        count[p] = s + 1
        i = first[p] + s
        table[NP * CAP + i] = t
        table[p * CAP + s] = i
        facts = jnp.where(lane == 1, 8 * offsets[1, t], jnp.where(lane == 2, 1, 0))
        meta[p, pl.ds(s, 1), :] = jnp.where(lane == 0, 8 * offsets[0, t], facts)
        return carry

    lax.fori_loop(0, NT, fill, 0)


def slots(routes, offsets):
    return pl.pallas_call(
        slot_kernel,
        out_shape=(
            jax.ShapeDtypeStruct((NP * CAP + NT,), jnp.int32),
            jax.ShapeDtypeStruct((NP, CAP, TS), jnp.int32),
        ),
        in_specs=[SMEM, SMEM],
        out_specs=(SMEM, VMEM),
        scratch_shapes=[pltpu.SMEM((NP,), jnp.int32), pltpu.SMEM((NP,), jnp.int32)],
        name="slots",
    )(routes, offsets)


def band(row):
    wide = jnp.broadcast_to(row, (TS, 2 * TS))
    return pltpu.roll(wide, 0, 1, stride=1, stride_axis=0)[:, :TS].astype(BF16)


def match_kernel(
    table, offsets, visits, counts, coefs, taps, meta, img_in, var_in, bad_in, wgt_out, num_out, facts_out,
    img, var, bad, weights, products, wslots, nslots, vert, horz, lm, rows, in_sem, own_sem, send_sem, recv_sem,
):
    x, y, z, core = place()
    loads = [
        pltpu.make_async_copy(src, dst, in_sem.at[i])
        for i, (src, dst) in enumerate(((var_in, var), (bad_in, bad), (img_in, img)))
    ]
    for load in loads:
        load.start()

    def along_x(step):
        return {"patch": y * 2 + lax.rem(core + step[1], 2), "visit": lax.rem(x + step[0], NA) * NZ + z}

    def along_y(step):
        return {"patch": patch_at(y, core, step)}

    for step in STEPS[:-1]:
        signal(along_x(step))
        signal(along_y(step))

    span = taps.shape[2]
    tap = lax.broadcasted_iota(jnp.int32, (span, 2 * TS), 0) - span // 2
    spot = lax.broadcasted_iota(jnp.int32, (span, 2 * TS), 1)
    spot = jnp.where(spot < TS, spot, spot - 2 * TS)
    down = jnp.dot(taps[:, 0, :], (spot == tap).astype(BF16), preferred_element_type=F32)
    across = jnp.dot(taps[:, 1, :], (spot == -tap).astype(BF16), preferred_element_type=F32)
    horz[...] = jnp.zeros_like(horz)
    for k in range(NB):
        vert[k * TS : (k + 1) * TS, :] = band(down[k : k + 1, :])
        half = slice((k % 2) * TS, (k % 2 + 1) * TS)
        horz[k // 2, half, half] = band(across[k : k + 1, :])
    level = lax.broadcasted_iota(jnp.int32, (NB, NB), 0)
    column = lax.broadcasted_iota(jnp.int32, (NB, NB), 1)
    for v in range(2):
        for c in range(3):
            used = (level == column) & (level < counts[v])
            diagonal = jnp.where(used, coefs[c, v : v + 1, :].astype(F32), 0.0).astype(BF16)
            rows[v, c] = jnp.dot(diagonal, jnp.ones((NB, TS), BF16), preferred_element_type=F32)
    loads[0].wait()
    loads[1].wait()

    def weigh(i, carry):
        t = table[NP * CAP + i]
        weights[i] = jnp.where(bad[t] == 0, 1.0 / var[t].astype(F32), 0.0).astype(BF16)
        return carry

    copies = []

    def to_patch(kind, r, begin=0, end=CAP):
        source, made, out = ((weights, wslots, wgt_out), (products, nslots, num_out))[kind]
        ring = x if kind == 0 else y
        there, here = patch_at(ring, core, STEPS[r]), ring * 2 + core

        def sort(j, carry):
            made[j] = source[table[j]]
            return carry

        lax.fori_loop(there * CAP + begin, there * CAP + end, sort, 0)
        tiles = made.at[pl.ds(there * CAP + begin, end - begin)], out.at[here, pl.ds(begin, end - begin)]
        pairs = [(0 if end == CAP else 1, *tiles)]
        if end == CAP:
            pairs.append((2, meta.at[there], facts_out.at[kind, here]))
        for i, src, dst in pairs:
            if r == NP - 1:
                copy = pltpu.make_async_copy(src, dst, own_sem.at[kind, i])
                copy.start()
            else:
                device = along_x(STEPS[r]) if kind == 0 else along_y(STEPS[r])
                copy = send(src, dst, send_sem.at[kind, i, r], recv_sem.at[kind, i, r], device)
            copies.append(copy)

    lax.fori_loop(0, CAP // 2, weigh, 0)
    loads[2].wait()

    row_iota = lax.broadcasted_iota(jnp.int32, (TS, TS), 0)
    col_iota = lax.broadcasted_iota(jnp.int32, (1, TS), 1)

    def pair(step, carry):
        ids = [table[NP * CAP + 2 * step + i] for i in range(2)]
        two = jnp.concatenate([img[ids[0]], img[ids[1]]], axis=1)
        own_visit = [visits[t] for t in ids]
        rho = [(row_iota + 8 * offsets[0, t]).astype(F32) * (1.0 / WIN) for t in ids]
        gamma = [(col_iota + 8 * offsets[1, t]).astype(F32) * (1.0 / WIN) for t in ids]
        for part in range(NB // 4):
            blurred = jnp.dot(
                vert[part * 4 * TS : (part + 1) * 4 * TS, :], two, preferred_element_type=F32
            )
            for kk in range(4):
                k = part * 4 + kk
                for i in range(2):
                    lm[i * TS : (i + 1) * TS, k * TS : (k + 1) * TS] = blurred[
                        kk * TS : (kk + 1) * TS, i * TS : (i + 1) * TS
                    ].astype(BF16)
        matched = [None, None]
        for kp in range(NB // 2):
            smooth = jnp.dot(lm[:, kp * 2 * TS : (kp + 1) * 2 * TS], horz[kp], preferred_element_type=F32)
            for kk in range(2):
                k = 2 * kp + kk
                for i in range(2):
                    a0, a1, a2 = (rows[own_visit[i], c, k : k + 1, :] for c in range(3))
                    term = (a1 * rho[i] + (a0 + a2 * gamma[i])) * smooth[
                        i * TS : (i + 1) * TS, kk * TS : (kk + 1) * TS
                    ]
                    matched[i] = term if matched[i] is None else matched[i] + term
        for i in range(2):
            weight = weights[2 * step + i].astype(F32)
            products[2 * step + i] = (weight * matched[i].astype(BF16).astype(F32)).astype(BF16)
        return carry

    lax.fori_loop(0, CAP // 4, pair, 0)
    wait(2 * (NP - 1))
    to_patch(1, 0, 0, CAP // 2)
    lax.fori_loop(CAP // 2, NT, weigh, 0)
    for r in range(2):
        to_patch(0, r)
    lax.fori_loop(CAP // 4, CAP // 2, pair, 0)
    to_patch(1, 0, CAP // 2)
    for r in range(2, NP):
        to_patch(0, r)
    for r in range(1, NT // CAP):
        lax.fori_loop(r * CAP // 2, (r + 1) * CAP // 2, pair, 0)
        if r < NT // CAP - 1:
            to_patch(1, r)
    for r in range(NT // CAP - 1, NP):
        to_patch(1, r)
    for copy in copies:
        copy.wait()


def match(*operands):
    dma = pltpu.SemaphoreType.DMA
    got = jax.ShapeDtypeStruct((NP, CAP, TS, TS), BF16)
    facts = jax.ShapeDtypeStruct((2, NP, CAP, TS), jnp.int32)
    return pl.pallas_call(
        match_kernel,
        out_shape=(got, got, facts),
        in_specs=[SMEM, SMEM, SMEM, SMEM, VMEM, VMEM, VMEM, HBM, HBM, HBM],
        out_specs=(ANY, ANY, ANY),
        scratch_shapes=[
            pltpu.VMEM((NT, TS, TS), BF16),
            pltpu.VMEM((NT, TS, TS), BF16),
            pltpu.VMEM((NT, TS, TS), jnp.int32),
            pltpu.VMEM((NT, TS, TS), BF16),
            pltpu.VMEM((NT, TS, TS), BF16),
            pltpu.VMEM((NP * CAP, TS, TS), BF16),
            pltpu.VMEM((NP * CAP, TS, TS), BF16),
            pltpu.VMEM((NB * TS, TS), BF16),
            pltpu.VMEM((NB // 2, 2 * TS, 2 * TS), BF16),
            pltpu.VMEM((2 * TS, NB * TS), BF16),
            pltpu.VMEM((2, 3, NB, TS), F32),
            dma((3,)), dma((2, 3)), dma((2, 3, NP)), dma((2, 3, NP)),
        ],
        compiler_params=pltpu.CompilerParams(
            collective_id=0, has_side_effects=True, vmem_limit_bytes=54 * 2**20
        ),
        name="match_tiles",
    )(*operands)


def add_kernel(
    facts_in, wgt, num, wgt_sum, num_sum, wgt_window, num_window, wgt_tiles, num_tiles, facts, facts_sem, sem
):
    planes = ((0, wgt_tiles, wgt_sum, wgt_window), (1, num_tiles, num_sum, num_window))

    def loads(source):
        part = pl.ds(pl.multiple_of(source * CAP, CAP), CAP)
        return (
            pltpu.make_async_copy(wgt.at[part], wgt_tiles.at[part], sem.at[0, source]),
            pltpu.make_async_copy(num.at[part], num_tiles.at[part], sem.at[1, source]),
        )

    facts_load = pltpu.make_async_copy(facts_in, facts, facts_sem)
    facts_load.start()
    for source in range(NP):
        for load in loads(source):
            load.start()

    def clear(i, carry):
        for plane in planes:
            plane[3][i] = jnp.zeros((WIN, TS), F32)
        return carry

    lax.fori_loop(0, WIN // TS + 1, clear, 0)
    facts_load.wait()
    lane = lax.broadcasted_iota(jnp.int32, (TS, TS), 1)

    def add(source, carry):
        arriving = loads(source)
        for kind, tiles, _, window in planes:
            arriving[kind].wait()
            work = []
            for s in range(CAP):
                j = source * CAP + s
                used = facts[kind, j, 2]
                top = pl.multiple_of(facts[kind, j, 0], 8)
                left = facts[kind, j, 1]
                shift = lax.rem(left, TS)
                tile = pltpu.roll(tiles[j].astype(F32), shift, 1)
                here = lane >= jnp.where(used > 0, shift, TS)
                there = lane < jnp.where(used > 0, shift, 0)
                work.append((left // TS, top, tile, here, there))
            for q, top, tile, here, there in work:
                window[q, pl.ds(top, TS), :] += jnp.where(here, tile, 0.0)
                window[q + 1, pl.ds(top, TS), :] += jnp.where(there, tile, 0.0)
        return carry

    lax.fori_loop(0, NP, add, 0)
    _, _, z, _ = place()

    def write(a, carry):
        for i, k in enumerate(BLOCKS):
            v = a * NZ + lax.rem(z + k, NZ)
            for half in range(2):
                at = pl.multiple_of((2 * v + half) * SIDE, SIDE)
                for _, _, out, window in planes:
                    for q in range(WIN // TS):
                        out[a, i, half, :, q * TS : (q + 1) * TS] = window[q, pl.ds(at, SIDE), :].astype(BF16)
        return carry

    lax.fori_loop(0, NA, write, 0)


def add_tiles(wgt, num, facts):
    out = jax.ShapeDtypeStruct((NA, NZ, 2, SIDE, WIN), BF16)
    tiles = [t.reshape(NP * CAP, TS, TS) for t in (wgt, num)]
    return pl.pallas_call(
        add_kernel,
        out_shape=(out, out),
        in_specs=[ANY, ANY, ANY],
        out_specs=(VMEM, VMEM),
        scratch_shapes=[pltpu.VMEM((WIN // TS + 1, WIN, TS), F32)] * 2
        + [pltpu.VMEM((NP * CAP, TS, TS), BF16)] * 2
        + [
            pltpu.SMEM((2, NP * CAP, TS), jnp.int32),
            pltpu.SemaphoreType.DMA,
            pltpu.SemaphoreType.DMA((2, NP)),
        ],
        compiler_params=pltpu.CompilerParams(vmem_limit_bytes=48 * 2**20),
        name="add_tiles",
    )(facts.reshape(2, NP * CAP, TS), *tiles)


class Plane:
    def __init__(self, a, z, along_a, along_z, owner_z, src, a_recv, a_send, mid, z_recv, z_send, as_sem, ar_sem, zs_sem, zr_sem):
        self.a, self.z, self.along_a, self.along_z, self.owner_z, self.src = a, z, along_a, along_z, owner_z, src
        self.a_recv, self.a_send, self.mid, self.z_recv, self.z_send = a_recv, a_send, mid, z_recv, z_send
        self.as_sem, self.ar_sem, self.zs_sem, self.zr_sem = as_sem, ar_sem, zs_sem, zr_sem
        self.copies = {}

    def pass_on(self, name, way, step, i, src, dst):
        to = self.along_a(lax.rem(self.a + (1, NA - 1)[way], NA))
        sems = self.as_sem.at[way, step, i], self.ar_sem.at[way, step, i]
        self.copies[name, way, i] = send(src, dst, *sems, to)

    def first(self, i):
        piece = FAR_PIECES[i]
        for way in range(2):
            there = self.src.at[lax.rem(self.a + 2, NA), piece, way]
            self.pass_on("far", way, 0, i, there, self.a_recv.at[way, 0, piece])

    def second(self, i):
        piece = PIECES[i]
        for f, far in enumerate(FAR_PIECES):
            if far.start == piece.start:
                for way in range(2):
                    self.copies["far", way, f].wait_recv()
        for way in range(2):
            to = lax.rem(self.a + (1, NA - 1)[way], NA)
            mine = self.src[to, piece, way].astype(F32)
            self.a_send[way, piece] = (mine + self.a_recv[way, 0, piece].astype(F32)).astype(BF16)
            self.pass_on("sum", way, 2, i, self.a_send.at[way, piece], self.a_recv.at[way, 2, piece])
            self.pass_on("raw", way, 1, i, self.src.at[to, piece, 1 - way], self.a_recv.at[way, 1, piece])

    def ready(self, i):
        for way in range(2):
            self.copies["raw", way, i].wait_recv()
            self.copies["sum", way, i].wait_recv()

    def ring_sum(self, at):
        return [
            self.src[self.a, at, half].astype(F32)
            + self.a_recv[half, 2, at].astype(F32)
            + self.a_recv[1 - half, 1, at].astype(F32)
            for half in range(2)
        ]

    def keep(self, at):
        for half, value in enumerate(self.ring_sum(at)):
            self.mid[at, half] = value.astype(BF16)

    def along(self, j):
        for way in range(2):
            at = BLOCKS.index(4 - j if way == 0 else 4 + j)
            to = (self.along_z if j < 3 else self.owner_z)(lax.rem(self.z + (1 if way == 0 else NZ - 1), NZ))
            if j == 0:
                src, dst = self.mid.at[at, way], self.z_recv.at[way, 0, way]
            else:
                src, dst = self.z_send.at[way, j - 1], self.z_recv.at[way, j]
                self.copies["z", way, j - 1].wait_recv()
                block, got = self.mid.at[at], self.z_recv.at[way, j - 1]
                src[way] = (block[way].astype(F32) + got[way].astype(F32)).astype(BF16)
                if j == 1:
                    src[1 - way] = block[1 - way]
                else:
                    src[1 - way] = (block[1 - way].astype(F32) + got[1 - way].astype(F32)).astype(BF16)
            self.copies["z", way, j] = send(src, dst, self.zs_sem.at[way, j], self.zr_sem.at[way, j], to)

    def total(self, out):
        for way in range(2):
            self.copies["z", way, 3].wait_recv()
            out = [value + self.z_recv[way, 3, half].astype(F32) for half, value in enumerate(out)]
        return jnp.concatenate(out, axis=0)

    def finish(self):
        for copy in self.copies.values():
            copy.wait_send()


PLANE_SCRATCH = 9


def plane_scratch():
    block = (2, SIDE, WIN)
    dma = pltpu.SemaphoreType.DMA
    return [
        pltpu.VMEM((2, 3, NZ, SIDE, WIN), BF16),
        pltpu.VMEM((2, NZ, SIDE, WIN), BF16),
        pltpu.VMEM((NZ,) + block, BF16),
        pltpu.VMEM((2, NZ // 2) + block, BF16),
        pltpu.VMEM((2, NZ // 2 - 1) + block, BF16),
        dma((2, 3, len(PIECES))), dma((2, 3, len(PIECES))), dma((2, NZ // 2)), dma((2, NZ // 2)),
    ]


def sum_kernel(wgt, num, coadd, depth, *scratch):
    x, y, z, core = place()
    along_x = lambda to: {"visit": to * NZ + z}
    along_y = lambda to: {"patch": to * 2 + core}
    along_z = lambda to: {"visit": x * NZ + to}
    swapped = lambda to: {"patch": x * 2 + core, "visit": y * NZ + to}
    kept, swap_send, swap_recv = scratch[2 * PLANE_SCRATCH :]

    for to in (1, NA - 1):
        signal(along_x(lax.rem(x + to, NA)))
        signal(along_y(lax.rem(y + to, NA)))
    for to in (1, NZ - 1):
        signal(along_z(lax.rem(z + to, NZ)))
        signal(swapped(lax.rem(z + to, NZ)))

    @pl.when(x != y)
    def _():
        signal(swapped(z))
        wait(9)

    @pl.when(x == y)
    def _():
        wait(8)

    planes = (
        Plane(y, z, along_y, along_z, swapped, wgt, *scratch[:PLANE_SCRATCH]),
        Plane(x, z, along_x, along_z, along_z, num, *scratch[PLANE_SCRATCH : 2 * PLANE_SCRATCH]),
    )
    for i in range(len(FAR_PIECES)):
        for plane in planes:
            plane.first(i)
    for i in range(len(PIECES)):
        for plane in planes:
            plane.second(i)
    for i in range(len(PIECES)):
        for plane in planes:
            plane.ready(i)
            for at in range(NZ - 1)[PIECES[i]]:
                plane.keep(at)
        if i < NZ // 2:
            for plane in planes:
                plane.along(i)
    planes[0].keep(NZ - 1)
    own = planes[0].mid.at[NZ - 1]
    swap = pltpu.make_async_remote_copy(
        src_ref=own, dst_ref=kept, send_sem=swap_send, recv_sem=swap_recv, device_id=swapped(z), device_id_type=MESH
    )

    @pl.when(x != y)
    def _():
        swap.start()

    @pl.when(x == y)
    def _():
        kept[...] = own[...]

    mine = planes[1].total(planes[1].ring_sum(NZ - 1))

    @pl.when(x != y)
    def _():
        swap.wait()

    total = planes[0].total([kept[half].astype(F32) for half in range(2)])
    depth[...] = total
    coadd[...] = mine / jnp.maximum(total, 1.0)
    for plane in planes:
        plane.finish()


def sum_windows(wgt, num):
    out = jax.ShapeDtypeStruct((2 * SIDE, WIN), F32)
    return pl.pallas_call(
        sum_kernel,
        out_shape=(out, out),
        in_specs=[VMEM, VMEM],
        out_specs=(VMEM, VMEM),
        scratch_shapes=plane_scratch()
        + plane_scratch()
        + [pltpu.VMEM((2, SIDE, WIN), BF16), pltpu.SemaphoreType.DMA, pltpu.SemaphoreType.DMA],
        compiler_params=pltpu.CompilerParams(
            collective_id=1, has_side_effects=True, vmem_limit_bytes=40 * 2**20
        ),
        name="sum_windows",
    )(wgt, num)


def local(images, variances, bad_pixels, routes, offsets, tile_visits, coefficients, kernel_counts, taps):
    routes, offsets, coefficients = routes.T, offsets.T, coefficients.transpose(1, 0, 2)
    table, meta = slots(routes, offsets)
    got = match(
        table, offsets, tile_visits, kernel_counts, coefficients, taps, meta, images, variances, bad_pixels
    )
    return sum_windows(*add_tiles(*got))


def solution(mesh):
    tiles = P(("patch", "visit"), None, None)
    return jax.shard_map(
        local,
        mesh=mesh,
        in_specs=(
            tiles, tiles, tiles,
            P(("patch", "visit"), None), P(("patch", "visit"), None), P(("patch", "visit")),
            P("visit", None, None), P("visit"), P(),
        ),
        out_specs=(P(("patch", "visit"), None), P(("patch", "visit"), None)),
        check_vma=False,
    )
```
